32 devices in a mesh: ctx: 8 (over y, x, core), head: 4 (over z).
Axes of the slice: x: 2, y: 2, z: 4, core: 2. Of those that a mesh axis runs over, the one named last changes fastest.
Arguments:
- queries: bfloat16 [1024, 4096], P('ctx', 'head')
- cache_keys: bfloat16 [8192, 8, 128], P('ctx', 'head')
- cache_values: bfloat16 [8192, 8, 128], P('ctx', 'head'), may hold values from -6 to 6
- shard_len: int32 [8], P('ctx'), may hold values from 256 to 1024, as said below
- out_proj: bfloat16 [4096, 4096], P('head'), may hold values from -0.5 to 0.5
- states: bfloat16 [1024, 4096], P('ctx', 'head'), may hold values from -6 to 6
- adapter_in: bfloat16 [4096, 128], P('head'), may hold values from -0.09375 to 0.09375
- adapter_out: bfloat16 [128, 4096], P(None, 'head'), may hold values from -0.5 to 0.5
Outputs:
- teacher: bfloat16 [1024, 4096], P('ctx', 'head')
- loss: float32 [], replicated
- grad_in: float32 [4096, 128], P('head')
- grad_out: float32 [128, 4096], P(None, 'head')
The draws below stay inside these ranges and needn't reach their ends.
Inputs may be any that keep to these rules, and one draw needn't show every extreme that they name: `shard_len`: the first block holds 1024 live positions.
All inputs are finite; a program needn't handle non-finite values.
Results may differ from the reference program's by a relative error of at most 0.012.
Values may be sent and summed in bfloat16 or wider, within the bound.
A program may use at most 64 MiB of HBM per device.

```python
import jax
import jax.numpy as jnp
from jax import lax

D = 4096
H = 32
KVH = 8
HD = 128
RANK = 128
CTX_DEV = 1024
ANS = 1024
NCTX = 8192
N_CTX = 8


def draw_queries(key, part):
    key = jax.random.fold_in(key, 1)
    base = 1.5 * jax.random.normal(key, (ANS, H, HD), jnp.float32)
    return base.reshape(ANS, H * HD).astype(jnp.bfloat16)


def draw_cache_keys(key, part):
    key = jax.random.fold_in(key, 2)
    base = jax.random.normal(key, (NCTX, KVH, HD), jnp.float32)
    return base.astype(jnp.bfloat16)


def draw_shard_len(key, part):
    key = jax.random.fold_in(key, 11)
    lengths = jax.random.randint(key, (N_CTX,), CTX_DEV // 4, CTX_DEV + 1, jnp.int32)
    return lengths.at[0].set(CTX_DEV)


def levels(stream_key, extent, cuts, low, top_value):
    loudness, own = 1.0, jax.random.fold_in(stream_key, 6)
    for axis_at, shards_of in cuts:
        draws = jnp.exp(jax.random.uniform(jax.random.fold_in(own, axis_at), (shards_of,), jnp.float32, low / len(cuts), top_value / len(cuts)))
        loudness = loudness * jnp.repeat(draws, extent[axis_at] // shards_of).reshape([-1 if axis == axis_at else 1 for axis in range(len(extent))])
    return loudness


def gaussian(key, dims, deviation, reach, shards=(), held_as=jnp.bfloat16):
    array = deviation * jax.random.normal(key, dims, jnp.float32)
    if shards:
        array = array * levels(key, dims, shards, -0.22, 0.18)
    return jnp.clip(array, -reach, reach).astype(held_as)


def setup_inputs(seed: int = 0) -> dict:
    key_list = jax.random.split(jax.random.key(seed), 9)
    return {
        "queries": draw_queries(jax.random.fold_in(key_list[8], 71), 0),
        "cache_keys": draw_cache_keys(jax.random.fold_in(key_list[8], 71), 0),
        "cache_values": gaussian(key_list[2], (NCTX, KVH, HD), 1.0, 6.0, ((0, 8), (1, 4))),
        "shard_len": draw_shard_len(jax.random.fold_in(key_list[8], 71), 0),
        "out_proj": gaussian(key_list[4], (H * HD, D), HD ** -0.5, 0.5, ((0, 4),)),
        "states": gaussian(key_list[5], (ANS, D), 1.0, 6.0, ((0, 8), (1, 4))),
        "adapter_in": gaussian(key_list[6], (D, RANK), D ** -0.5, 0.09375, ((0, 4),)),
        "adapter_out": gaussian(key_list[7], (RANK, D), RANK ** -0.5, 0.5, ((1, 4),)),
    }


def reference(queries, cache_keys, cache_values, shard_len, out_proj, states, adapter_in, adapter_out):
    group = H // KVH
    scale = HD ** (-0.5)
    qry = queries.astype(jnp.float32).reshape(ANS, KVH, group, HD)
    keys_all = cache_keys.reshape(N_CTX, CTX_DEV, KVH, HD)
    vals_all = cache_values.reshape(N_CTX, CTX_DEV, KVH, HD)

    def step(carry, blockdata):
        top, total, accum = carry
        kblk, vblk, live = blockdata
        valid = jnp.arange(CTX_DEV, dtype=jnp.int32) < live
        score = jnp.einsum('rkgd,nkd->rkgn', qry, kblk.astype(jnp.float32)) * scale
        score = jnp.where(valid, score, jnp.float32(-1e+30))
        mblk = lax.optimization_barrier(jnp.max(score, axis=-1))
        prob = jnp.where(valid, jnp.exp(score - mblk[..., None]), jnp.float32(0.0)).astype(jnp.bfloat16)
        lblk = lax.optimization_barrier(jnp.sum(prob.astype(jnp.float32), axis=-1))
        oblk = jnp.einsum('rkgn,nkd->rkgd', prob.astype(jnp.float32), vblk.astype(jnp.float32))
        normed = (oblk / lblk[..., None]).astype(jnp.bfloat16).astype(jnp.float32)
        newtop = jnp.maximum(top, mblk)
        wold = jnp.exp(top - newtop)
        wnew = lblk * jnp.exp(mblk - newtop)
        total = total * wold + wnew
        accum = accum * wold[..., None] + normed * wnew[..., None]
        return ((newtop, total, accum), None)
    init = (jnp.full((ANS, KVH, group), -1e+30, jnp.float32), jnp.zeros((ANS, KVH, group), jnp.float32), jnp.zeros((ANS, KVH, group, HD), jnp.float32))
    (top, total, accum), _ = lax.scan(step, init, (keys_all, vals_all, shard_len))
    attn = (accum / total[..., None]).reshape(ANS, H * HD).astype(jnp.bfloat16)
    teacher = jnp.dot(attn, out_proj, preferred_element_type=jnp.float32).astype(jnp.bfloat16)
    hidden = jnp.dot(states, adapter_in, preferred_element_type=jnp.float32)
    active = jax.nn.silu(hidden).astype(jnp.bfloat16)
    diff = jnp.dot(active, adapter_out, preferred_element_type=jnp.float32) - teacher.astype(jnp.float32)
    loss = jnp.sum(diff * diff) / (ANS * D)
    cotan = (diff / jnp.sqrt(jnp.float32(ANS))).astype(jnp.bfloat16)
    grad_out = jnp.dot(active.T, cotan, preferred_element_type=jnp.float32)
    back = jnp.dot(cotan, adapter_out.T, preferred_element_type=jnp.float32)
    sig = jax.nn.sigmoid(hidden)
    inner = (back * sig * (1.0 + hidden * (1.0 - sig))).astype(jnp.bfloat16)
    grad_in = jnp.dot(states.T, inner, preferred_element_type=jnp.float32)
    return (teacher, loss, grad_in, grad_out)
```

```python
import functools
import math

import jax
import jax.numpy as jnp
from jax import lax
from jax.experimental import pallas as pl
from jax.experimental.pallas import tpu as pltpu
from jax.sharding import PartitionSpec as P

F32 = jnp.float32
BF16 = jnp.bfloat16
LANES = 128
CHUNK_ROWS = 16


def dot(a, b, dims=((1,), (0,))):
    return lax.dot_general(a, b, (dims, ((), ())), preferred_element_type=F32)


def remote(src, dst, send, recv, **where):
    return pltpu.make_async_remote_copy(
        src_ref=src, dst_ref=dst, send_sem=send, recv_sem=recv, device_id=where,
        device_id_type=pl.DeviceIdType.MESH,
    )


def kernel(
    nctx, nhead, kv, unit, total_rows, total_width,
    q_ref, k_ref, vt_ref, op_hbm, st_ref, ai_ref, ao_ref,
    teacher_ref, loss_ref, gi_ref, go_ref,
    op, qbuf, mine, mine_ml, part, part_ml, sib_a, sib_ml, merged, merged_ml, recv_a, recv_ml,
    attn, z_out, z_in, hbuf, bbuf, st_all, g_all, l_all, gpart, gred, gfull,
    op_sem, q_send, q_fwd, q_recv, p_send, p_recv, m_send, m_recv, z_send, z_recv,
    h_send, h_recv, b_send, b_recv, s_send, s_fwd, s_recv, g_send, g_recv, l_send, l_recv,
    r_send, r_recv, a_send, a_recv,
):
    c = lax.axis_index("ctx")
    z = lax.axis_index("head")
    chips = nctx // 2
    chip = c // 2
    par = c % 2
    sib = c + 1 - 2 * par
    rows, width = q_ref.shape
    heads = width // LANES
    group = heads // kv

    def peer(i):
        other, bit = 0, 1
        while bit < chips:
            other = other + bit * (((chip // bit) % 2 + (i // bit) % 2) % 2)
            bit *= 2
        return 2 * other + par

    barrier = pltpu.get_barrier_semaphore()

    def greet(k, _):
        pl.semaphore_signal(
            barrier, inc=1, device_id={"ctx": (c + k) % nctx}, device_id_type=pl.DeviceIdType.MESH
        )
        return 0

    def greet_head(k, _):
        pl.semaphore_signal(
            barrier, inc=1, device_id={"head": (z + k) % nhead}, device_id_type=pl.DeviceIdType.MESH
        )
        return 0

    load_op = pltpu.make_async_copy(op_hbm, op, op_sem)
    load_op.start()
    lax.fori_loop(1, nctx, greet, 0)
    lax.fori_loop(1, nhead, greet_head, 0)
    pl.semaphore_wait(barrier, nctx + nhead - 2)

    def loop(low, high, f):
        def step(i, _):
            f(i)
            return 0

        lax.fori_loop(low, high, step, 0)

    def q_direct(i):
        return remote(q_ref, qbuf.at[i, 0], q_send.at[i], q_recv.at[i, 0], ctx=peer(i))

    def q_sib():
        return remote(q_ref, qbuf.at[0, 1], q_send.at[0], q_recv.at[0, 1], ctx=sib)

    def q_forward(i):
        return remote(qbuf.at[i, 0], qbuf.at[i, 1], q_fwd.at[i], q_recv.at[i, 1], ctx=sib)

    q_sib().start()
    loop(1, chips, lambda i: q_direct(i).start())

    def h_copy(k):
        return remote(hbuf.at[z], hbuf.at[z], h_send.at[k], h_recv.at[k], head=(z + k) % nhead)

    def h_in(k):
        return remote(
            hbuf.at[(z - k + nhead) % nhead], hbuf.at[(z - k + nhead) % nhead],
            h_send.at[k], h_recv.at[k], head=(z + k) % nhead,
        )

    hbuf[z] = dot(st_ref[...], ai_ref[...])
    loop(1, nhead, lambda k: h_copy(k).start())

    qbuf[0, 0] = q_ref[...]
    own_rows = pl.ds(pl.multiple_of(c * rows, rows), rows)
    st_all[own_rows, :] = st_ref[...]

    one_hot = jnp.where(
        lax.broadcasted_iota(jnp.int32, (2 * rows, LANES), 1) == 0, 1.0, 0.0
    ).astype(BF16)

    def attend(i, j, out, out_ml):
        for n in range(kv):
            keys = k_ref[n]
            vals = vt_ref[n]
            for g in range(0, group, 2):
                h = n * group + g
                pair = jnp.concatenate(
                    [
                        qbuf[i, j, :, h * LANES : (h + 1) * LANES],
                        qbuf[i, j, :, (h + 1) * LANES : (h + 2) * LANES],
                    ],
                    axis=0,
                )
                score = dot(keys, jnp.concatenate([pair, one_hot], axis=1), ((1,), (1,)))
                top = jnp.max(score, axis=0, keepdims=True)
                prob = jnp.exp2((score - top) * unit).astype(BF16)
                acc = dot(vals, prob)
                tot = acc[LANES : LANES + 1, :]
                norm = (acc[:LANES, :] / tot).astype(BF16)
                for e in range(2):
                    cut = slice(e * rows, (e + 1) * rows)
                    out[i, (h + e) * LANES : (h + e + 1) * LANES, :] = norm[:, cut]
                    out_ml[i, 0, h + e : h + e + 1, :] = top[:, cut]
                    out_ml[i, 1, h + e : h + e + 1, :] = tot[:, cut]

    def p_copy(i):
        return (
            remote(part.at[i], sib_a.at[i], p_send.at[i, 0], p_recv.at[i, 0], ctx=sib),
            remote(part_ml.at[i], sib_ml.at[i], p_send.at[i, 1], p_recv.at[i, 1], ctx=sib),
        )

    def m_copy(i):
        return (
            remote(merged.at[i], recv_a.at[i], m_send.at[i, 0], m_recv.at[i, 0], ctx=peer(i)),
            remote(merged_ml.at[i], recv_ml.at[i], m_send.at[i, 1], m_recv.at[i, 1], ctx=peer(i)),
        )

    def merge(i):
        for copy in p_copy(i):
            copy.wait_recv()
        m0, l0 = mine_ml[i, 0, :heads, :], mine_ml[i, 1, :heads, :]
        m1, l1 = sib_ml[i, 0, :heads, :], sib_ml[i, 1, :heads, :]
        top = jnp.maximum(m0, m1)
        w0 = l0 * jnp.exp2((m0 - top) * unit)
        w1 = l1 * jnp.exp2((m1 - top) * unit)
        tot = w0 + w1
        merged_ml[i, 0, :heads, :] = top
        merged_ml[i, 1, :heads, :] = tot
        f0, f1 = w0 / tot, w1 / tot
        for h in range(heads):
            cut = slice(h * LANES, (h + 1) * LANES)
            merged[i, cut, :] = (
                mine[i, cut, :].astype(F32) * f0[h : h + 1, :]
                + sib_a[i, cut, :].astype(F32) * f1[h : h + 1, :]
            ).astype(BF16)

        @pl.when(i > 0)
        def _():
            for copy in m_copy(i):
                copy.start()

    def chip_step(i):
        @pl.when(i > 0)
        def _():
            q_direct(i).wait_recv()
            q_forward(i).start()

        attend(i, 0, mine, mine_ml)
        q_forward(i).wait_recv()
        attend(i, 1, part, part_ml)
        for copy in p_copy(i):
            copy.start()

        @pl.when(i > 0)
        def _():
            merge(i - 1)

    loop(0, chips, chip_step)
    merge(chips - 1)

    loop(1, nhead, lambda k: h_in(k).wait_recv())
    hidden = hbuf[0]
    for k in range(1, nhead):
        hidden = hidden + hbuf[k]
    sig = jax.nn.sigmoid(hidden)
    active32 = (hidden * sig).astype(BF16).astype(F32)
    active = active32.astype(BF16)
    active_t = active32.T.astype(BF16)

    def wait_partials(i):
        for copy in m_copy(i):
            copy.wait_recv()

    loop(1, chips, wait_partials)

    def s_direct(i):
        return remote(st_ref, st_all.at[own_rows], s_send.at[i], s_recv.at[i, 0], ctx=peer(i))

    def s_sib():
        return remote(st_ref, st_all.at[own_rows], s_send.at[0], s_recv.at[0, 1], ctx=sib)

    def s_forward(i):
        its = pl.ds(pl.multiple_of(peer(i) * rows, rows), rows)
        return remote(st_all.at[its], st_all.at[its], s_fwd.at[i], s_recv.at[i, 1], ctx=sib)

    def s_in(i):
        its = pl.ds(pl.multiple_of(peer(i) * rows, rows), rows)
        return remote(st_ref, st_all.at[its], s_send.at[i], s_recv.at[i, 0], ctx=peer(i))

    def s_in_sib(i):
        owner = peer(i) + 1 - 2 * par
        its = pl.ds(pl.multiple_of(owner * rows, rows), rows)
        return remote(st_ref, st_all.at[its], s_send.at[i], s_recv.at[i, 1], ctx=sib)

    s_sib().start()
    loop(1, chips, lambda i: s_direct(i).start())

    tops = [merged_ml[0, 0, :heads, :]] + [recv_ml[i, 0, :heads, :] for i in range(1, chips)]
    tots = [merged_ml[0, 1, :heads, :]] + [recv_ml[i, 1, :heads, :] for i in range(1, chips)]
    top = functools.reduce(jnp.maximum, tops)
    weights = [t * jnp.exp2((m - top) * unit) for m, t in zip(tops, tots)]
    whole = functools.reduce(jnp.add, weights)
    weights = [w / whole for w in weights]
    for h in range(heads):
        cut = slice(h * LANES, (h + 1) * LANES)
        acc = merged[0, cut, :].astype(F32) * weights[0][h : h + 1, :]
        for i in range(1, chips):
            acc = acc + recv_a[i, cut, :].astype(F32) * weights[i][h : h + 1, :]
        attn[:, cut] = acc.T.astype(BF16)

    load_op.wait()

    def z_copy(k):
        return remote(z_out.at[k], z_in.at[k], z_send.at[k], z_recv.at[k], head=(z + k) % nhead)

    def project(owner):
        cols = pl.ds(pl.multiple_of(owner * width, width), width)
        return dot(attn[...], op[:, cols])

    def z_step(k):
        z_out[k] = project((z + k) % nhead).astype(BF16)
        z_copy(k).start()

    loop(1, nhead, z_step)
    own = project(z)
    student = dot(active, ao_ref[...])

    def s_relay(i):
        s_in(i).wait_recv()
        s_forward(i).start()

    loop(1, chips, s_relay)
    loop(1, nhead, lambda k: z_copy(k).wait_recv())
    for k in range(1, nhead):
        own = own + z_in[k].astype(F32)
    teacher = own.astype(BF16)
    teacher_ref[...] = teacher
    diff = student - teacher.astype(F32)
    cotan = (diff * (1.0 / math.sqrt(total_rows))).astype(BF16)

    bbuf[z, :rows, :] = dot(cotan, ao_ref[...], ((1,), (1,)))
    square = diff * diff
    lane = square[:, :LANES]
    for n in range(1, width // LANES):
        lane = lane + square[:, n * LANES : (n + 1) * LANES]
    bbuf[z, rows : rows + 8, :] = jnp.sum(lane.reshape(rows // 8, 8, LANES), axis=0)

    def b_copy(k):
        return remote(bbuf.at[z], bbuf.at[z], b_send.at[k], b_recv.at[k], head=(z + k) % nhead)

    def b_in(k):
        src = (z - k + nhead) % nhead
        return remote(bbuf.at[src], bbuf.at[src], b_send.at[k], b_recv.at[k], head=(z + k) % nhead)

    loop(1, nhead, lambda k: b_copy(k).start())

    cw = width * (gpart.shape[0] // CHUNK_ROWS) // nctx
    ncol = width // cw

    def chunk(ref, d):
        return ref.at[
            pl.ds(pl.multiple_of((d // ncol) * CHUNK_ROWS, CHUNK_ROWS), CHUNK_ROWS),
            pl.ds(pl.multiple_of((d % ncol) * cw, cw), cw),
        ]

    gpart[...] = dot(active_t, cotan).astype(BF16)

    def r_copy(k):
        d = (c + k) % nctx
        return remote(chunk(gpart, d), gred.at[c], r_send.at[k], r_recv.at[k], ctx=d)

    def r_in(k):
        src = (c - k + nctx) % nctx
        return remote(chunk(gpart, c), gred.at[src], r_send.at[k], r_recv.at[k], ctx=src)

    loop(1, nctx, lambda k: r_copy(k).start())
    gred[c] = chunk(gpart, c)[...]

    loop(1, nhead, lambda k: b_in(k).wait_recv())
    back = bbuf[0]
    for k in range(1, nhead):
        back = back + bbuf[k]
    g_all[own_rows, :] = (
        back[:rows] * sig * (1.0 + hidden * (1.0 - sig))
    ).astype(BF16)
    l_all[c] = back[rows : rows + 8]

    def g_copy(k):
        d = (c + k) % nctx
        return (
            remote(g_all.at[own_rows], g_all.at[own_rows], g_send.at[k], g_recv.at[k], ctx=d),
            remote(l_all.at[c], l_all.at[c], l_send.at[k], l_recv.at[k], ctx=d),
        )

    def g_in(k):
        src = (c - k + nctx) % nctx
        its = pl.ds(pl.multiple_of(src * rows, rows), rows)
        return (
            remote(g_all.at[its], g_all.at[its], g_send.at[k], g_recv.at[k], ctx=src),
            remote(l_all.at[src], l_all.at[src], l_send.at[k], l_recv.at[k], ctx=src),
        )

    def g_start(k):
        for copy in g_copy(k):
            copy.start()

    loop(1, nctx, g_start)

    loop(1, nctx, lambda k: r_in(k).wait_recv())
    total = gred[0].astype(F32)
    for k in range(1, nctx):
        total = total + gred[k].astype(F32)
    chunk(gfull, c)[...] = total.astype(BF16)

    def a_copy(k):
        d = (c + k) % nctx
        return remote(chunk(gfull, c), chunk(gfull, c), a_send.at[k], a_recv.at[k], ctx=d)

    def a_in(k):
        src = (c - k + nctx) % nctx
        return remote(chunk(gfull, src), chunk(gfull, src), a_send.at[k], a_recv.at[k], ctx=src)

    loop(1, nctx, lambda k: a_copy(k).start())

    loop(0, chips, lambda i: s_in_sib(i).wait_recv())

    def g_wait(k):
        for copy in g_in(k):
            copy.wait_recv()

    loop(1, nctx, g_wait)
    inner_t = g_all[...].astype(F32).T.astype(BF16)
    gi_ref[...] = dot(inner_t, st_all[...]).T
    squares = l_all[0]
    for k in range(1, nctx):
        squares = squares + l_all[k]
    loss = jnp.sum(jnp.sum(squares, axis=0, keepdims=True), axis=1, keepdims=True)
    loss_ref[...] = loss / (total_rows * total_width)

    loop(1, nctx, lambda k: a_in(k).wait_recv())
    go_ref[...] = gfull[...].astype(F32)

    q_sib().wait_send()
    s_sib().wait_send()
    p_wait = lambda i: [copy.wait_send() for copy in p_copy(i)] and None
    loop(0, chips, p_wait)

    def chips_sent(i):
        q_direct(i).wait_send()
        q_forward(i).wait_send()
        s_direct(i).wait_send()
        s_forward(i).wait_send()
        for copy in m_copy(i):
            copy.wait_send()

    loop(1, chips, chips_sent)

    def head_sent(k):
        h_copy(k).wait_send()
        z_copy(k).wait_send()
        b_copy(k).wait_send()

    loop(1, nhead, head_sent)

    def ctx_sent(k):
        r_copy(k).wait_send()
        a_copy(k).wait_send()
        for copy in g_copy(k):
            copy.wait_send()

    loop(1, nctx, ctx_sent)


def shards(queries, cache_keys, cache_values, shard_len, out_proj, states, adapter_in, adapter_out):
    nctx, nhead = lax.axis_size("ctx"), lax.axis_size("head")
    rows, width = queries.shape
    length, kv, hd = cache_keys.shape
    rank = adapter_in.shape[1]
    chips = nctx // 2
    unit = hd ** (-0.5) * math.log2(math.e)
    live = jnp.arange(length, dtype=jnp.int32) < shard_len[0]
    bias = jnp.where(live, 0.0, -1e30).astype(BF16)
    first = jnp.arange(hd) == 0
    keys = jnp.transpose(cache_keys, (1, 0, 2))
    extra = jnp.where(first[None, :], bias[:, None], jnp.zeros((), BF16))
    keys = jnp.concatenate([keys, jnp.broadcast_to(extra[None], keys.shape)], axis=2)
    vals = jnp.transpose(cache_values, (1, 2, 0))
    vals = jnp.concatenate([vals, jnp.ones((kv, CHUNK_ROWS, length), BF16)], axis=1)
    hpad = -(-(width // LANES) // 8) * 8
    dma = pltpu.SemaphoreType.DMA
    vmem = pl.BlockSpec(memory_space=pltpu.VMEM)
    cw = width * (rank // CHUNK_ROWS) // nctx
    scratch = [
        pltpu.VMEM(out_proj.shape, BF16),
        pltpu.VMEM((chips, 2, rows, width), BF16),
        pltpu.VMEM((chips, width, rows), BF16),
        pltpu.VMEM((chips, 2, hpad, rows), F32),
        pltpu.VMEM((chips, width, rows), BF16),
        pltpu.VMEM((chips, 2, hpad, rows), F32),
        pltpu.VMEM((chips, width, rows), BF16),
        pltpu.VMEM((chips, 2, hpad, rows), F32),
        pltpu.VMEM((chips, width, rows), BF16),
        pltpu.VMEM((chips, 2, hpad, rows), F32),
        pltpu.VMEM((chips, width, rows), BF16),
        pltpu.VMEM((chips, 2, hpad, rows), F32),
        pltpu.VMEM((rows, width), BF16),
        pltpu.VMEM((nhead, rows, width), BF16),
        pltpu.VMEM((nhead, rows, width), BF16),
        pltpu.VMEM((nhead, rows, rank), F32),
        pltpu.VMEM((nhead, rows + 8, rank), F32),
        pltpu.VMEM((nctx * rows, width), BF16),
        pltpu.VMEM((nctx * rows, rank), BF16),
        pltpu.VMEM((nctx, 8, LANES), F32),
        pltpu.VMEM((rank, width), BF16),
        pltpu.VMEM((nctx, CHUNK_ROWS, cw), BF16),
        pltpu.VMEM((rank, width), BF16),
        dma,
        dma((chips,)), dma((chips,)), dma((chips, 2)),
        dma((chips, 2)), dma((chips, 2)),
        dma((chips, 2)), dma((chips, 2)),
        dma((nhead,)), dma((nhead,)),
        dma((nhead,)), dma((nhead,)),
        dma((nhead,)), dma((nhead,)),
        dma((chips,)), dma((chips,)), dma((chips, 2)),
        dma((nctx,)), dma((nctx,)), dma((nctx,)), dma((nctx,)),
        dma((nctx,)), dma((nctx,)), dma((nctx,)), dma((nctx,)),
    ]
    teacher, loss, grad_in, grad_out = pl.pallas_call(
        functools.partial(
            kernel, nctx, nhead, kv, unit, rows * nctx, width * nhead
        ),
        out_shape=(
            jax.ShapeDtypeStruct((rows, width), BF16),
            jax.ShapeDtypeStruct((1, 1), F32),
            jax.ShapeDtypeStruct((width, rank), F32),
            jax.ShapeDtypeStruct((rank, width), F32),
        ),
        in_specs=[vmem, vmem, vmem, pl.BlockSpec(memory_space=pl.ANY), vmem, vmem, vmem],
        out_specs=(vmem, vmem, vmem, vmem),
        scratch_shapes=scratch,
        compiler_params=pltpu.CompilerParams(
            collective_id=0, has_side_effects=True, vmem_limit_bytes=50 * 2**20
        ),
    )(queries, keys, vals, out_proj, states, adapter_in, adapter_out)
    return (teacher, loss.reshape(()), grad_in, grad_out)


def solution(mesh):
    placed = (
        P("ctx", "head"),
        P("ctx", "head", None),
        P("ctx", "head", None),
        P("ctx"),
        P("head", None),
        P("ctx", "head"),
        P("head", None),
        P(None, "head"),
    )
    return jax.shard_map(
        shards,
        mesh=mesh,
        in_specs=placed,
        out_specs=(P("ctx", "head"), P(), P("head", None), P(None, "head")),
        check_vma=False,
    )
```

```python
import functools
import math

import jax
import jax.numpy as jnp
from jax import lax
from jax.experimental import pallas as pl
from jax.experimental.pallas import tpu as pltpu
from jax.sharding import PartitionSpec as P

F32 = jnp.float32
BF16 = jnp.bfloat16
LANES = 128
CHUNK_ROWS = 16


def dot(a, b, dims=((1,), (0,))):
    return lax.dot_general(a, b, (dims, ((), ())), preferred_element_type=F32)


def remote(src, dst, send, recv, **where):
    return pltpu.make_async_remote_copy(
        src_ref=src, dst_ref=dst, send_sem=send, recv_sem=recv, device_id=where,
        device_id_type=pl.DeviceIdType.MESH,
    )


def kernel(
    nctx, nhead, kv, unit, total_rows, total_width,
    q_ref, k_ref, vt_ref, op_hbm, st_ref, ai_ref, ao_ref,
    teacher_ref, loss_ref, gi_ref, go_ref,
    op, qbuf, mine, mine_ml, part, part_ml, sib_a, sib_ml, merged, merged_ml, recv_a, recv_ml,
    attn, own_z, z_out, z_in, hbuf, bbuf, lbuf, st_all, g_all, l_all, gpart, gred, gfull,
    op_sem, q_send, q_fwd, q_recv, p_send, p_recv, m_send, m_recv, z_send, z_recv,
    h_send, h_recv, b_send, b_recv, s_send, s_fwd, s_recv, g_send, g_recv, l_send, l_recv,
    r_send, r_recv, a_send, a_recv,
):
    c = lax.axis_index("ctx")
    z = lax.axis_index("head")
    chips = nctx // 2
    chip = c // 2
    par = c % 2
    sib = c + 1 - 2 * par
    rows, width = q_ref.shape
    heads = width // LANES
    group = heads // kv

    def peer(i):
        other, bit = 0, 1
        while bit < chips:
            other = other + bit * (((chip // bit) % 2 + (i // bit) % 2) % 2)
            bit *= 2
        return 2 * other + par

    barrier = pltpu.get_barrier_semaphore()

    def greet(k, _):
        pl.semaphore_signal(
            barrier, inc=1, device_id={"ctx": (c + k) % nctx}, device_id_type=pl.DeviceIdType.MESH
        )
        return 0

    def greet_head(k, _):
        pl.semaphore_signal(
            barrier, inc=1, device_id={"head": (z + k) % nhead}, device_id_type=pl.DeviceIdType.MESH
        )
        return 0

    load_op = pltpu.make_async_copy(op_hbm, op, op_sem)
    load_op.start()
    lax.fori_loop(1, nctx, greet, 0)
    lax.fori_loop(1, nhead, greet_head, 0)
    pl.semaphore_wait(barrier, nctx + nhead - 2)

    def loop(low, high, f):
        def step(i, _):
            f(i)
            return 0

        lax.fori_loop(low, high, step, 0)

    hrows = rows // 2
    wide = group * hrows

    def half(a):
        return pl.ds(a * hrows, hrows)

    def q_direct(a, i):
        return remote(
            q_ref.at[half(a)], qbuf.at[a, i, 0], q_send.at[a, i], q_recv.at[a, i, 0], ctx=peer(i)
        )

    def q_sib(a):
        return remote(
            q_ref.at[half(a)], qbuf.at[a, 0, 1], q_send.at[a, 0], q_recv.at[a, 0, 1], ctx=sib
        )

    def q_forward(a, i):
        return remote(
            qbuf.at[a, i, 0], qbuf.at[a, i, 1], q_fwd.at[a, i], q_recv.at[a, i, 1], ctx=sib
        )

    def q_start(a):
        q_sib(a).start()
        loop(1, chips, lambda i: q_direct(a, i).start())

    q_start(0)
    qbuf[0, 0, 0] = q_ref[:hrows, :]
    qbuf[1, 0, 0] = q_ref[hrows:, :]

    def h_copy(k):
        return remote(hbuf.at[z], hbuf.at[z], h_send.at[k], h_recv.at[k], head=(z + k) % nhead)

    def h_in(k):
        return remote(
            hbuf.at[(z - k + nhead) % nhead], hbuf.at[(z - k + nhead) % nhead],
            h_send.at[k], h_recv.at[k], head=(z + k) % nhead,
        )

    own_rows = pl.ds(pl.multiple_of(c * rows, rows), rows)

    one_hot = jnp.where(
        lax.broadcasted_iota(jnp.int32, (wide, LANES), 1) == 0, 1.0, 0.0
    ).astype(BF16)

    def scores(a, i, j, n):
        block = jnp.concatenate(
            [
                qbuf[a, i, j, :, (n * group + g) * LANES : (n * group + g + 1) * LANES]
                for g in range(group)
            ],
            axis=0,
        )
        return dot(k_ref[n], jnp.concatenate([block, one_hot], axis=1), ((1,), (1,)))

    def weigh(score, a, i, n, out, out_ml):
        top = jnp.max(score, axis=0, keepdims=True)
        prob = jnp.exp2((score - top) * unit).astype(BF16)
        acc = dot(vt_ref[n], prob)
        tot = acc[LANES : LANES + 1, :]
        out[a, i, n * LANES : (n + 1) * LANES, :] = (acc[:LANES, :] / tot).astype(BF16)
        out_ml[a, i, 0, n : n + 1, :] = top
        out_ml[a, i, 1, n : n + 1, :] = tot

    def p_copy(a, i):
        return (
            remote(part.at[a, i], sib_a.at[a, i], p_send.at[a, i, 0], p_recv.at[a, i, 0], ctx=sib),
            remote(
                part_ml.at[a, i], sib_ml.at[a, i], p_send.at[a, i, 1], p_recv.at[a, i, 1], ctx=sib
            ),
        )

    def m_copy(a, i):
        return (
            remote(
                merged.at[a, i], recv_a.at[a, i], m_send.at[a, i, 0], m_recv.at[a, i, 0],
                ctx=peer(i),
            ),
            remote(
                merged_ml.at[a, i], recv_ml.at[a, i], m_send.at[a, i, 1], m_recv.at[a, i, 1],
                ctx=peer(i),
            ),
        )

    def merge(a, i):
        for copy in p_copy(a, i):
            copy.wait_recv()
        m0, l0 = mine_ml[a, i, 0, :kv, :], mine_ml[a, i, 1, :kv, :]
        m1, l1 = sib_ml[a, i, 0, :kv, :], sib_ml[a, i, 1, :kv, :]
        top = jnp.maximum(m0, m1)
        w0 = l0 * jnp.exp2((m0 - top) * unit)
        w1 = l1 * jnp.exp2((m1 - top) * unit)
        tot = w0 + w1
        merged_ml[a, i, 0, :kv, :] = top
        merged_ml[a, i, 1, :kv, :] = tot
        f0, f1 = w0 / tot, w1 / tot
        for n in range(kv):
            cut = slice(n * LANES, (n + 1) * LANES)
            merged[a, i, cut, :] = (
                mine[a, i, cut, :].astype(F32) * f0[n : n + 1, :]
                + sib_a[a, i, cut, :].astype(F32) * f1[n : n + 1, :]
            ).astype(BF16)

        @pl.when(i > 0)
        def _():
            for copy in m_copy(a, i):
                copy.start()

    def z_copy(a, k):
        return remote(
            z_out.at[a, k], z_in.at[a, k], z_send.at[a, k], z_recv.at[a, k], head=(z + k) % nhead
        )

    def combine(a):
        tops = [merged_ml[a, 0, 0, :kv, :]] + [recv_ml[a, i, 0, :kv, :] for i in range(1, chips)]
        tots = [merged_ml[a, 0, 1, :kv, :]] + [recv_ml[a, i, 1, :kv, :] for i in range(1, chips)]
        top = functools.reduce(jnp.maximum, tops)
        weights = [t * jnp.exp2((m - top) * unit) for m, t in zip(tops, tots)]
        whole = functools.reduce(jnp.add, weights)
        weights = [w / whole for w in weights]
        for n in range(kv):
            cut = slice(n * LANES, (n + 1) * LANES)
            acc = merged[a, 0, cut, :].astype(F32) * weights[0][n : n + 1, :]
            for i in range(1, chips):
                acc = acc + recv_a[a, i, cut, :].astype(F32) * weights[i][n : n + 1, :]
            turned = acc.T.astype(BF16)
            for g in range(group):
                h = n * group + g
                attn[a, :, h * LANES : (h + 1) * LANES] = turned[g * hrows : (g + 1) * hrows, :]

        def project(owner):
            cols = pl.ds(pl.multiple_of(owner * width, width), width)
            return dot(attn[a], op[:, cols])

        def z_step(k):
            z_out[a, k] = project((z + k) % nhead).astype(BF16)
            z_copy(a, k).start()

        loop(1, nhead, z_step)
        own_z[a] = project(z)

    def partials_in(a):
        def wait(i):
            for copy in m_copy(a, i):
                copy.wait_recv()

        loop(1, chips, wait)

    def chip_step(a, i):
        @pl.when(i > 0)
        def _():
            q_direct(a, i).wait_recv()
            q_forward(a, i).start()

        todo = [(0, n) for n in range(kv)] + [(1, n) for n in range(kv)]
        ahead = scores(a, i, *todo[0])
        for at, (j, n) in enumerate(todo):
            score = ahead
            if at + 1 < len(todo):
                if at + 1 == kv:
                    q_forward(a, i).wait_recv()
                ahead = scores(a, i, *todo[at + 1])
            weigh(score, a, i, n, *((part, part_ml) if j else (mine, mine_ml)))
        for copy in p_copy(a, i):
            copy.start()

        if a == 0:
            @pl.when(i > 0)
            def _():
                merge(0, i - 1)

            @pl.when(i == 1)
            def _():
                q_start(1)
        else:
            @pl.when(i == 0)
            def _():
                merge(0, chips - 1)

            @pl.when(i > 0)
            def _():
                merge(1, i - 1)

            @pl.when(i == chips // 2)
            def _():
                partials_in(0)
                load_op.wait()
                combine(0)

    loop(0, chips, lambda i: chip_step(0, i))

    hbuf[z] = dot(st_ref[...], ai_ref[...])
    loop(1, nhead, lambda k: h_copy(k).start())
    st_all[own_rows, :] = st_ref[...]

    loop(0, chips, lambda i: chip_step(1, i))
    merge(1, chips - 1)

    loop(1, nhead, lambda k: h_in(k).wait_recv())
    hidden = hbuf[0]
    for k in range(1, nhead):
        hidden = hidden + hbuf[k]
    sig = jax.nn.sigmoid(hidden)
    active32 = (hidden * sig).astype(BF16).astype(F32)
    active = active32.astype(BF16)
    active_t = active32.T.astype(BF16)

    partials_in(1)

    def s_direct(i):
        return remote(st_ref, st_all.at[own_rows], s_send.at[i], s_recv.at[i, 0], ctx=peer(i))

    def s_sib():
        return remote(st_ref, st_all.at[own_rows], s_send.at[0], s_recv.at[0, 1], ctx=sib)

    def s_forward(i):
        its = pl.ds(pl.multiple_of(peer(i) * rows, rows), rows)
        return remote(st_all.at[its], st_all.at[its], s_fwd.at[i], s_recv.at[i, 1], ctx=sib)

    def s_in(i):
        its = pl.ds(pl.multiple_of(peer(i) * rows, rows), rows)
        return remote(st_ref, st_all.at[its], s_send.at[i], s_recv.at[i, 0], ctx=peer(i))

    def s_in_sib(i):
        owner = peer(i) + 1 - 2 * par
        its = pl.ds(pl.multiple_of(owner * rows, rows), rows)
        return remote(st_ref, st_all.at[its], s_send.at[i], s_recv.at[i, 1], ctx=sib)

    s_sib().start()
    loop(1, chips, lambda i: s_direct(i).start())

    combine(1)
    student = dot(active, ao_ref[...])

    def s_relay(i):
        s_in(i).wait_recv()
        s_forward(i).start()

    loop(1, chips, s_relay)
    for a in range(2):
        loop(1, nhead, lambda k: z_copy(a, k).wait_recv())
        own = own_z[a]
        for k in range(1, nhead):
            own = own + z_in[a, k].astype(F32)
        teacher_ref[a * hrows : (a + 1) * hrows, :] = own.astype(BF16)
    diff = student - teacher_ref[...].astype(F32)
    cotan = (diff * (1.0 / math.sqrt(total_rows))).astype(BF16)

    bbuf[z] = dot(cotan, ao_ref[...], ((1,), (1,))).astype(BF16)
    square = diff * diff
    lane = square[:, :LANES]
    for n in range(1, width // LANES):
        lane = lane + square[:, n * LANES : (n + 1) * LANES]
    lbuf[z] = jnp.sum(lane.reshape(rows // 8, 8, LANES), axis=0)

    def b_copy(k):
        to = (z + k) % nhead
        return (
            remote(bbuf.at[z], bbuf.at[z], b_send.at[k, 0], b_recv.at[k, 0], head=to),
            remote(lbuf.at[z], lbuf.at[z], b_send.at[k, 1], b_recv.at[k, 1], head=to),
        )

    def b_in(k):
        src = (z - k + nhead) % nhead
        return (
            remote(bbuf.at[src], bbuf.at[src], b_send.at[k, 0], b_recv.at[k, 0], head=src),
            remote(lbuf.at[src], lbuf.at[src], b_send.at[k, 1], b_recv.at[k, 1], head=src),
        )

    def b_start(k):
        for copy in b_copy(k):
            copy.start()

    loop(1, nhead, b_start)

    cw = width * (gpart.shape[0] // CHUNK_ROWS) // nctx
    ncol = width // cw

    def chunk(ref, d):
        return ref.at[
            pl.ds(pl.multiple_of((d // ncol) * CHUNK_ROWS, CHUNK_ROWS), CHUNK_ROWS),
            pl.ds(pl.multiple_of((d % ncol) * cw, cw), cw),
        ]

    gpart[...] = dot(active_t, cotan).astype(BF16)

    def r_copy(k):
        d = (c + k) % nctx
        return remote(chunk(gpart, d), gred.at[c], r_send.at[k], r_recv.at[k], ctx=d)

    def r_in(k):
        src = (c - k + nctx) % nctx
        return remote(chunk(gpart, c), gred.at[src], r_send.at[k], r_recv.at[k], ctx=src)

    loop(1, nctx, lambda k: r_copy(k).start())
    gred[c] = chunk(gpart, c)[...]

    def b_wait(k):
        for copy in b_in(k):
            copy.wait_recv()

    loop(1, nhead, b_wait)
    back, squares = bbuf[0].astype(F32), lbuf[0]
    for k in range(1, nhead):
        back = back + bbuf[k].astype(F32)
        squares = squares + lbuf[k]
    g_all[own_rows, :] = (
        back * sig * (1.0 + hidden * (1.0 - sig))
    ).astype(BF16)
    l_all[c] = squares

    def g_copy(k):
        d = (c + k) % nctx
        return (
            remote(g_all.at[own_rows], g_all.at[own_rows], g_send.at[k], g_recv.at[k], ctx=d),
            remote(l_all.at[c], l_all.at[c], l_send.at[k], l_recv.at[k], ctx=d),
        )

    def g_in(k):
        src = (c - k + nctx) % nctx
        its = pl.ds(pl.multiple_of(src * rows, rows), rows)
        return (
            remote(g_all.at[its], g_all.at[its], g_send.at[k], g_recv.at[k], ctx=src),
            remote(l_all.at[src], l_all.at[src], l_send.at[k], l_recv.at[k], ctx=src),
        )

    def g_start(k):
        for copy in g_copy(k):
            copy.start()

    loop(1, nctx, g_start)

    loop(1, nctx, lambda k: r_in(k).wait_recv())
    total = gred[0].astype(F32)
    for k in range(1, nctx):
        total = total + gred[k].astype(F32)
    chunk(gfull, c)[...] = total.astype(BF16)

    def a_copy(k):
        d = (c + k) % nctx
        return remote(chunk(gfull, c), chunk(gfull, c), a_send.at[k], a_recv.at[k], ctx=d)

    def a_in(k):
        src = (c - k + nctx) % nctx
        return remote(chunk(gfull, src), chunk(gfull, src), a_send.at[k], a_recv.at[k], ctx=src)

    loop(1, nctx, lambda k: a_copy(k).start())

    loop(0, chips, lambda i: s_in_sib(i).wait_recv())

    def g_wait(k):
        for copy in g_in(k):
            copy.wait_recv()

    loop(1, nctx, g_wait)
    inner_t = g_all[...].astype(F32).T.astype(BF16)
    gi_ref[...] = dot(inner_t, st_all[...])
    squares = l_all[0]
    for k in range(1, nctx):
        squares = squares + l_all[k]
    loss = jnp.sum(jnp.sum(squares, axis=0, keepdims=True), axis=1, keepdims=True)
    loss_ref[...] = loss / (total_rows * total_width)

    loop(1, nctx, lambda k: a_in(k).wait_recv())
    go_ref[...] = gfull[...]

    s_sib().wait_send()
    for a in range(2):
        q_sib(a).wait_send()

        def p_sent(i):
            for copy in p_copy(a, i):
                copy.wait_send()

        loop(0, chips, p_sent)

        def chips_sent(i):
            q_direct(a, i).wait_send()
            q_forward(a, i).wait_send()
            for copy in m_copy(a, i):
                copy.wait_send()

        loop(1, chips, chips_sent)
        loop(1, nhead, lambda k: z_copy(a, k).wait_send())

    def states_sent(i):
        s_direct(i).wait_send()
        s_forward(i).wait_send()

    loop(1, chips, states_sent)

    def head_sent(k):
        h_copy(k).wait_send()
        for copy in b_copy(k):
            copy.wait_send()

    loop(1, nhead, head_sent)

    def ctx_sent(k):
        r_copy(k).wait_send()
        a_copy(k).wait_send()
        for copy in g_copy(k):
            copy.wait_send()

    loop(1, nctx, ctx_sent)


def shards(queries, cache_keys, cache_values, shard_len, out_proj, states, adapter_in, adapter_out):
    nctx, nhead = lax.axis_size("ctx"), lax.axis_size("head")
    rows, width = queries.shape
    length, kv, hd = cache_keys.shape
    rank = adapter_in.shape[1]
    chips = nctx // 2
    unit = hd ** (-0.5) * math.log2(math.e)
    live = jnp.arange(length, dtype=jnp.int32) < shard_len[0]
    bias = jnp.where(live, 0.0, -1e30).astype(BF16)
    first = jnp.arange(hd) == 0
    keys = jnp.transpose(cache_keys, (1, 0, 2))
    extra = jnp.where(first[None, :], bias[:, None], jnp.zeros((), BF16))
    keys = jnp.concatenate([keys, jnp.broadcast_to(extra[None], keys.shape)], axis=2)
    vals = jnp.transpose(cache_values, (1, 2, 0))
    vals = jnp.concatenate([vals, jnp.ones((kv, CHUNK_ROWS, length), BF16)], axis=1)
    hrows = rows // 2
    wide = width // LANES // kv * hrows
    dma = pltpu.SemaphoreType.DMA
    vmem = pl.BlockSpec(memory_space=pltpu.VMEM)
    cw = width * (rank // CHUNK_ROWS) // nctx
    blocks = [
        pltpu.VMEM((2, chips, kv * LANES, wide), BF16),
        pltpu.VMEM((2, chips, 2, 8, wide), F32),
    ]
    scratch = [
        pltpu.VMEM(out_proj.shape, BF16),
        pltpu.VMEM((2, chips, 2, hrows, width), BF16),
        *(blocks * 5),
        pltpu.VMEM((2, hrows, width), BF16),
        pltpu.VMEM((2, hrows, width), F32),
        pltpu.VMEM((2, nhead, hrows, width), BF16),
        pltpu.VMEM((2, nhead, hrows, width), BF16),
        pltpu.VMEM((nhead, rows, rank), F32),
        pltpu.VMEM((nhead, rows, rank), BF16),
        pltpu.VMEM((nhead, 8, LANES), F32),
        pltpu.VMEM((nctx * rows, width), BF16),
        pltpu.VMEM((nctx * rows, rank), BF16),
        pltpu.VMEM((nctx, 8, LANES), F32),
        pltpu.VMEM((rank, width), BF16),
        pltpu.VMEM((nctx, CHUNK_ROWS, cw), BF16),
        pltpu.VMEM((rank, width), BF16),
        dma,
        dma((2, chips)), dma((2, chips)), dma((2, chips, 2)),
        dma((2, chips, 2)), dma((2, chips, 2)),
        dma((2, chips, 2)), dma((2, chips, 2)),
        dma((2, nhead)), dma((2, nhead)),
        dma((nhead,)), dma((nhead,)),
        dma((nhead, 2)), dma((nhead, 2)),
        dma((chips,)), dma((chips,)), dma((chips, 2)),
        dma((nctx,)), dma((nctx,)), dma((nctx,)), dma((nctx,)),
        dma((nctx,)), dma((nctx,)), dma((nctx,)), dma((nctx,)),
    ]
    teacher, loss, grad_in, grad_out = pl.pallas_call(
        functools.partial(
            kernel, nctx, nhead, kv, unit, rows * nctx, width * nhead
        ),
        out_shape=(
            jax.ShapeDtypeStruct((rows, width), BF16),
            jax.ShapeDtypeStruct((1, 1), F32),
            jax.ShapeDtypeStruct((rank, width), F32),
            jax.ShapeDtypeStruct((rank, width), BF16),
        ),
        in_specs=[vmem, vmem, vmem, pl.BlockSpec(memory_space=pl.ANY), vmem, vmem, vmem],
        out_specs=(vmem, vmem, vmem, vmem),
        scratch_shapes=scratch,
        compiler_params=pltpu.CompilerParams(
            collective_id=0, has_side_effects=True, vmem_limit_bytes=50 * 2**20
        ),
    )(queries, keys, vals, out_proj, states, adapter_in, adapter_out)
    return (teacher, loss.reshape(()), grad_in.T, grad_out.astype(F32))


def solution(mesh):
    placed = (
        P("ctx", "head"),
        P("ctx", "head", None),
        P("ctx", "head", None),
        P("ctx"),
        P("head", None),
        P("ctx", "head"),
        P("head", None),
        P(None, "head"),
    )
    return jax.shard_map(
        shards,
        mesh=mesh,
        in_specs=placed,
        out_specs=(P("ctx", "head"), P(), P("head", None), P(None, "head")),
        check_vma=False,
    )
```

```python
import functools
import math

import jax
import jax.numpy as jnp
from jax import lax
from jax.experimental import pallas as pl
from jax.experimental.pallas import tpu as pltpu
from jax.sharding import PartitionSpec as P

F32 = jnp.float32
BF16 = jnp.bfloat16
LANES = 128
CHUNK_ROWS = 16


def dot(a, b, dims=((1,), (0,))):
    return lax.dot_general(a, b, (dims, ((), ())), preferred_element_type=F32)


def remote(src, dst, send, recv, **where):
    return pltpu.make_async_remote_copy(
        src_ref=src, dst_ref=dst, send_sem=send, recv_sem=recv, device_id=where,
        device_id_type=pl.DeviceIdType.MESH,
    )


def kernel(
    nctx, nhead, kv, unit, total_rows, total_width,
    q_ref, k_ref, vt_ref, op_hbm, st_ref, ai_ref, ao_ref,
    teacher_ref, loss_ref, gi_ref, go_ref,
    op, qbuf, mine, mine_ml, part, part_ml, sib_a, sib_ml, merged, merged_ml, recv_a, recv_ml,
    attn, own_z, z_out, z_in, hbuf, bbuf, lbuf, st_all, g_all, l_all, gpart, gred, gfull,
    op_sem, q_send, q_fwd, q_recv, p_send, p_recv, m_send, m_recv, z_send, z_recv,
    h_send, h_recv, b_send, b_recv, s_send, s_fwd, s_recv, g_send, g_recv, l_send, l_recv,
    r_send, r_recv, a_send, a_recv,
):
    c = lax.axis_index("ctx")
    z = lax.axis_index("head")
    chips = nctx // 2
    chip = c // 2
    par = c % 2
    sib = c + 1 - 2 * par
    rows, width = q_ref.shape
    heads = width // LANES
    group = heads // kv

    def peer(i):
        other, bit = 0, 1
        while bit < chips:
            other = other + bit * (((chip // bit) % 2 + (i // bit) % 2) % 2)
            bit *= 2
        return 2 * other + par

    barrier = pltpu.get_barrier_semaphore()

    def greet(k, _):
        pl.semaphore_signal(
            barrier, inc=1, device_id={"ctx": (c + k) % nctx}, device_id_type=pl.DeviceIdType.MESH
        )
        return 0

    def greet_head(k, _):
        pl.semaphore_signal(
            barrier, inc=1, device_id={"head": (z + k) % nhead}, device_id_type=pl.DeviceIdType.MESH
        )
        return 0

    load_op = pltpu.make_async_copy(op_hbm, op, op_sem)
    load_op.start()
    lax.fori_loop(1, nctx, greet, 0)
    lax.fori_loop(1, nhead, greet_head, 0)
    pl.semaphore_wait(barrier, nctx + nhead - 2)

    def loop(low, high, f):
        def step(i, _):
            f(i)
            return 0

        lax.fori_loop(low, high, step, 0)

    hrows = rows // 2
    wide = group * hrows

    def half(a):
        return pl.ds(a * hrows, hrows)

    def q_direct(a, i):
        return remote(
            q_ref.at[half(a)], qbuf.at[a, i, 0], q_send.at[a, i], q_recv.at[a, i, 0], ctx=peer(i)
        )

    def q_sib(a):
        return remote(
            q_ref.at[half(a)], qbuf.at[a, 0, 1], q_send.at[a, 0], q_recv.at[a, 0, 1], ctx=sib
        )

    def q_forward(a, i):
        return remote(
            qbuf.at[a, i, 0], qbuf.at[a, i, 1], q_fwd.at[a, i], q_recv.at[a, i, 1], ctx=sib
        )

    def q_start(a):
        q_sib(a).start()
        loop(1, chips, lambda i: q_direct(a, i).start())

    q_start(0)
    qbuf[0, 0, 0] = q_ref[:hrows, :]
    qbuf[1, 0, 0] = q_ref[hrows:, :]

    def h_copy(k):
        return remote(hbuf.at[z], hbuf.at[z], h_send.at[k], h_recv.at[k], head=(z + k) % nhead)

    def h_in(k):
        return remote(
            hbuf.at[(z - k + nhead) % nhead], hbuf.at[(z - k + nhead) % nhead],
            h_send.at[k], h_recv.at[k], head=(z + k) % nhead,
        )

    own_rows = pl.ds(pl.multiple_of(c * rows, rows), rows)

    one_hot = jnp.where(
        lax.broadcasted_iota(jnp.int32, (wide, LANES), 1) == 0, 1.0, 0.0
    ).astype(BF16)

    def scores(a, i, j, n):
        block = jnp.concatenate(
            [
                qbuf[a, i, j, :, (n * group + g) * LANES : (n * group + g + 1) * LANES]
                for g in range(group)
            ],
            axis=0,
        )
        return dot(k_ref[n], jnp.concatenate([block, one_hot], axis=1), ((1,), (1,)))

    def weigh(score, a, i, n, out, out_ml):
        top = jnp.max(score, axis=0, keepdims=True)
        prob = jnp.exp2((score - top) * unit).astype(BF16)
        acc = dot(vt_ref[n], prob)
        tot = acc[LANES : LANES + 1, :]
        out[a, i, n * LANES : (n + 1) * LANES, :] = (acc[:LANES, :] / tot).astype(BF16)
        out_ml[a, i, 0, n : n + 1, :] = top
        out_ml[a, i, 1, n : n + 1, :] = tot

    def p_copy(a, i):
        return (
            remote(part.at[a, i], sib_a.at[a, i], p_send.at[a, i, 0], p_recv.at[a, i, 0], ctx=sib),
            remote(
                part_ml.at[a, i], sib_ml.at[a, i], p_send.at[a, i, 1], p_recv.at[a, i, 1], ctx=sib
            ),
        )

    def m_copy(a, i):
        return (
            remote(
                merged.at[a, i], recv_a.at[a, i], m_send.at[a, i, 0], m_recv.at[a, i, 0],
                ctx=peer(i),
            ),
            remote(
                merged_ml.at[a, i], recv_ml.at[a, i], m_send.at[a, i, 1], m_recv.at[a, i, 1],
                ctx=peer(i),
            ),
        )

    def merge(a, i):
        for copy in p_copy(a, i):
            copy.wait_recv()
        m0, l0 = mine_ml[a, i, 0, :kv, :], mine_ml[a, i, 1, :kv, :]
        m1, l1 = sib_ml[a, i, 0, :kv, :], sib_ml[a, i, 1, :kv, :]
        top = jnp.maximum(m0, m1)
        w0 = l0 * jnp.exp2((m0 - top) * unit)
        w1 = l1 * jnp.exp2((m1 - top) * unit)
        tot = w0 + w1
        merged_ml[a, i, 0, :kv, :] = top
        merged_ml[a, i, 1, :kv, :] = tot
        f0, f1 = w0 / tot, w1 / tot
        for n in range(kv):
            cut = slice(n * LANES, (n + 1) * LANES)
            merged[a, i, cut, :] = (
                mine[a, i, cut, :].astype(F32) * f0[n : n + 1, :]
                + sib_a[a, i, cut, :].astype(F32) * f1[n : n + 1, :]
            ).astype(BF16)

        @pl.when(i > 0)
        def _():
            for copy in m_copy(a, i):
                copy.start()

    def z_copy(a, k):
        return remote(
            z_out.at[a, k], z_in.at[a, k], z_send.at[a, k], z_recv.at[a, k], head=(z + k) % nhead
        )

    def combine(a):
        tops = [merged_ml[a, 0, 0, :kv, :]] + [recv_ml[a, i, 0, :kv, :] for i in range(1, chips)]
        tots = [merged_ml[a, 0, 1, :kv, :]] + [recv_ml[a, i, 1, :kv, :] for i in range(1, chips)]
        top = functools.reduce(jnp.maximum, tops)
        weights = [t * jnp.exp2((m - top) * unit) for m, t in zip(tops, tots)]
        whole = functools.reduce(jnp.add, weights)
        weights = [w / whole for w in weights]
        for n in range(kv):
            cut = slice(n * LANES, (n + 1) * LANES)
            acc = merged[a, 0, cut, :].astype(F32) * weights[0][n : n + 1, :]
            for i in range(1, chips):
                acc = acc + recv_a[a, i, cut, :].astype(F32) * weights[i][n : n + 1, :]
            turned = acc.T.astype(BF16)
            for g in range(group):
                h = n * group + g
                attn[a, :, h * LANES : (h + 1) * LANES] = turned[g * hrows : (g + 1) * hrows, :]

        def project(owner):
            cols = pl.ds(pl.multiple_of(owner * width, width), width)
            return dot(attn[a], op[:, cols])

        def z_step(k):
            z_out[a, k] = project((z + k) % nhead).astype(BF16)
            z_copy(a, k).start()

        loop(1, nhead, z_step)
        own_z[a] = project(z)

    def partials_in(a):
        def wait(i):
            for copy in m_copy(a, i):
                copy.wait_recv()

        loop(1, chips, wait)

    def chip_step(a, i):
        @pl.when(i > 0)
        def _():
            q_direct(a, i).wait_recv()
            q_forward(a, i).start()

        todo = [(0, n) for n in range(kv)] + [(1, n) for n in range(kv)]
        ahead = scores(a, i, *todo[0])
        for at, (j, n) in enumerate(todo):
            score = ahead
            if at + 1 < len(todo):
                if at + 1 == kv:
                    q_forward(a, i).wait_recv()
                ahead = scores(a, i, *todo[at + 1])
            weigh(score, a, i, n, *((part, part_ml) if j else (mine, mine_ml)))
        for copy in p_copy(a, i):
            copy.start()

        if a == 0:
            @pl.when(i > 0)
            def _():
                merge(0, i - 1)

            @pl.when(i == 0)
            def _():
                q_start(1)
        else:
            @pl.when(i == chips - 1)
            def _():
                merge(0, chips - 1)

            @pl.when(i < chips - 1)
            def _():
                merge(1, i + 1)

            @pl.when(i == chips // 2 - 1)
            def _():
                partials_in(0)
                load_op.wait()
                combine(0)

    loop(0, chips, lambda i: chip_step(0, i))

    hbuf[z] = dot(st_ref[...], ai_ref[...])
    loop(1, nhead, lambda k: h_copy(k).start())
    st_all[own_rows, :] = st_ref[...]

    loop(0, chips, lambda t: chip_step(1, chips - 1 - t))
    merge(1, 0)

    loop(1, nhead, lambda k: h_in(k).wait_recv())
    hidden = hbuf[0]
    for k in range(1, nhead):
        hidden = hidden + hbuf[k]
    sig = jax.nn.sigmoid(hidden)
    active32 = (hidden * sig).astype(BF16).astype(F32)
    active = active32.astype(BF16)
    active_t = active32.T.astype(BF16)

    partials_in(1)

    def s_direct(i):
        return remote(st_ref, st_all.at[own_rows], s_send.at[i], s_recv.at[i, 0], ctx=peer(i))

    def s_sib():
        return remote(st_ref, st_all.at[own_rows], s_send.at[0], s_recv.at[0, 1], ctx=sib)

    def s_forward(i):
        its = pl.ds(pl.multiple_of(peer(i) * rows, rows), rows)
        return remote(st_all.at[its], st_all.at[its], s_fwd.at[i], s_recv.at[i, 1], ctx=sib)

    def s_in(i):
        its = pl.ds(pl.multiple_of(peer(i) * rows, rows), rows)
        return remote(st_ref, st_all.at[its], s_send.at[i], s_recv.at[i, 0], ctx=peer(i))

    def s_in_sib(i):
        owner = peer(i) + 1 - 2 * par
        its = pl.ds(pl.multiple_of(owner * rows, rows), rows)
        return remote(st_ref, st_all.at[its], s_send.at[i], s_recv.at[i, 1], ctx=sib)

    s_sib().start()
    loop(1, chips, lambda i: s_direct(i).start())

    combine(1)
    student = dot(active, ao_ref[...])

    def s_relay(i):
        s_in(i).wait_recv()
        s_forward(i).start()

    loop(1, chips, s_relay)
    for a in range(2):
        loop(1, nhead, lambda k: z_copy(a, k).wait_recv())
        own = own_z[a]
        for k in range(1, nhead):
            own = own + z_in[a, k].astype(F32)
        teacher_ref[a * hrows : (a + 1) * hrows, :] = own.astype(BF16)
    diff = student - teacher_ref[...].astype(F32)
    cotan = (diff * (1.0 / math.sqrt(total_rows))).astype(BF16)

    bbuf[z] = dot(cotan, ao_ref[...], ((1,), (1,))).astype(BF16)
    square = diff * diff
    lane = square[:, :LANES]
    for n in range(1, width // LANES):
        lane = lane + square[:, n * LANES : (n + 1) * LANES]
    lbuf[z] = jnp.sum(lane.reshape(rows // 8, 8, LANES), axis=0)

    def b_copy(k):
        to = (z + k) % nhead
        return (
            remote(bbuf.at[z], bbuf.at[z], b_send.at[k, 0], b_recv.at[k, 0], head=to),
            remote(lbuf.at[z], lbuf.at[z], b_send.at[k, 1], b_recv.at[k, 1], head=to),
        )

    def b_in(k):
        src = (z - k + nhead) % nhead
        return (
            remote(bbuf.at[src], bbuf.at[src], b_send.at[k, 0], b_recv.at[k, 0], head=src),
            remote(lbuf.at[src], lbuf.at[src], b_send.at[k, 1], b_recv.at[k, 1], head=src),
        )

    def b_start(k):
        for copy in b_copy(k):
            copy.start()

    loop(1, nhead, b_start)

    cw = width * (gpart.shape[0] // CHUNK_ROWS) // nctx
    ncol = width // cw

    def chunk(ref, d):
        return ref.at[
            pl.ds(pl.multiple_of((d // ncol) * CHUNK_ROWS, CHUNK_ROWS), CHUNK_ROWS),
            pl.ds(pl.multiple_of((d % ncol) * cw, cw), cw),
        ]

    gpart[...] = dot(active_t, cotan).astype(BF16)

    def r_copy(k):
        d = (c + k) % nctx
        return remote(chunk(gpart, d), gred.at[c], r_send.at[k], r_recv.at[k], ctx=d)

    def r_in(k):
        src = (c - k + nctx) % nctx
        return remote(chunk(gpart, c), gred.at[src], r_send.at[k], r_recv.at[k], ctx=src)

    loop(1, nctx, lambda k: r_copy(k).start())
    gred[c] = chunk(gpart, c)[...]

    def b_wait(k):
        for copy in b_in(k):
            copy.wait_recv()

    loop(1, nhead, b_wait)
    back, squares = bbuf[0].astype(F32), lbuf[0]
    for k in range(1, nhead):
        back = back + bbuf[k].astype(F32)
        squares = squares + lbuf[k]
    g_all[own_rows, :] = (
        back * sig * (1.0 + hidden * (1.0 - sig))
    ).astype(BF16)
    l_all[c] = squares

    def g_copy(k):
        d = (c + k) % nctx
        return (
            remote(g_all.at[own_rows], g_all.at[own_rows], g_send.at[k], g_recv.at[k], ctx=d),
            remote(l_all.at[c], l_all.at[c], l_send.at[k], l_recv.at[k], ctx=d),
        )

    def g_in(k):
        src = (c - k + nctx) % nctx
        its = pl.ds(pl.multiple_of(src * rows, rows), rows)
        return (
            remote(g_all.at[its], g_all.at[its], g_send.at[k], g_recv.at[k], ctx=src),
            remote(l_all.at[src], l_all.at[src], l_send.at[k], l_recv.at[k], ctx=src),
        )

    def g_start(k):
        for copy in g_copy(k):
            copy.start()

    loop(1, nctx, g_start)

    loop(1, nctx, lambda k: r_in(k).wait_recv())
    total = gred[0].astype(F32)
    for k in range(1, nctx):
        total = total + gred[k].astype(F32)
    chunk(gfull, c)[...] = total.astype(BF16)

    def a_copy(k):
        d = (c + k) % nctx
        return remote(chunk(gfull, c), chunk(gfull, c), a_send.at[k], a_recv.at[k], ctx=d)

    def a_in(k):
        src = (c - k + nctx) % nctx
        return remote(chunk(gfull, src), chunk(gfull, src), a_send.at[k], a_recv.at[k], ctx=src)

    loop(1, nctx, lambda k: a_copy(k).start())

    loop(0, chips, lambda i: s_in_sib(i).wait_recv())

    def g_wait(k):
        for copy in g_in(k):
            copy.wait_recv()

    loop(1, nctx, g_wait)
    inner_t = g_all[...].astype(F32).T.astype(BF16)
    gi_ref[...] = dot(inner_t, st_all[...])
    squares = l_all[0]
    for k in range(1, nctx):
        squares = squares + l_all[k]
    loss = jnp.sum(jnp.sum(squares, axis=0, keepdims=True), axis=1, keepdims=True)
    loss_ref[...] = loss / (total_rows * total_width)

    loop(1, nctx, lambda k: a_in(k).wait_recv())
    go_ref[...] = gfull[...]

    s_sib().wait_send()
    for a in range(2):
        q_sib(a).wait_send()

        def p_sent(i):
            for copy in p_copy(a, i):
                copy.wait_send()

        loop(0, chips, p_sent)

        def chips_sent(i):
            q_direct(a, i).wait_send()
            q_forward(a, i).wait_send()
            for copy in m_copy(a, i):
                copy.wait_send()

        loop(1, chips, chips_sent)
        loop(1, nhead, lambda k: z_copy(a, k).wait_send())

    def states_sent(i):
        s_direct(i).wait_send()
        s_forward(i).wait_send()

    loop(1, chips, states_sent)

    def head_sent(k):
        h_copy(k).wait_send()
        for copy in b_copy(k):
            copy.wait_send()

    loop(1, nhead, head_sent)

    def ctx_sent(k):
        r_copy(k).wait_send()
        a_copy(k).wait_send()
        for copy in g_copy(k):
            copy.wait_send()

    loop(1, nctx, ctx_sent)


def shards(queries, cache_keys, cache_values, shard_len, out_proj, states, adapter_in, adapter_out):
    nctx, nhead = lax.axis_size("ctx"), lax.axis_size("head")
    rows, width = queries.shape
    length, kv, hd = cache_keys.shape
    rank = adapter_in.shape[1]
    chips = nctx // 2
    unit = hd ** (-0.5) * math.log2(math.e)
    live = jnp.arange(length, dtype=jnp.int32) < shard_len[0]
    bias = jnp.where(live, 0.0, -1e30).astype(BF16)
    first = jnp.arange(hd) == 0
    keys = jnp.transpose(cache_keys, (1, 0, 2))
    extra = jnp.where(first[None, :], bias[:, None], jnp.zeros((), BF16))
    keys = jnp.concatenate([keys, jnp.broadcast_to(extra[None], keys.shape)], axis=2)
    vals = jnp.transpose(cache_values, (1, 2, 0))
    vals = jnp.concatenate([vals, jnp.ones((kv, CHUNK_ROWS, length), BF16)], axis=1)
    hrows = rows // 2
    wide = width // LANES // kv * hrows
    dma = pltpu.SemaphoreType.DMA
    vmem = pl.BlockSpec(memory_space=pltpu.VMEM)
    cw = width * (rank // CHUNK_ROWS) // nctx
    blocks = [
        pltpu.VMEM((2, chips, kv * LANES, wide), BF16),
        pltpu.VMEM((2, chips, 2, 8, wide), F32),
    ]
    scratch = [
        pltpu.VMEM(out_proj.shape, BF16),
        pltpu.VMEM((2, chips, 2, hrows, width), BF16),
        *(blocks * 5),
        pltpu.VMEM((2, hrows, width), BF16),
        pltpu.VMEM((2, hrows, width), F32),
        pltpu.VMEM((2, nhead, hrows, width), BF16),
        pltpu.VMEM((2, nhead, hrows, width), BF16),
        pltpu.VMEM((nhead, rows, rank), F32),
        pltpu.VMEM((nhead, rows, rank), BF16),
        pltpu.VMEM((nhead, 8, LANES), F32),
        pltpu.VMEM((nctx * rows, width), BF16),
        pltpu.VMEM((nctx * rows, rank), BF16),
        pltpu.VMEM((nctx, 8, LANES), F32),
        pltpu.VMEM((rank, width), BF16),
        pltpu.VMEM((nctx, CHUNK_ROWS, cw), BF16),
        pltpu.VMEM((rank, width), BF16),
        dma,
        dma((2, chips)), dma((2, chips)), dma((2, chips, 2)),
        dma((2, chips, 2)), dma((2, chips, 2)),
        dma((2, chips, 2)), dma((2, chips, 2)),
        dma((2, nhead)), dma((2, nhead)),
        dma((nhead,)), dma((nhead,)),
        dma((nhead, 2)), dma((nhead, 2)),
        dma((chips,)), dma((chips,)), dma((chips, 2)),
        dma((nctx,)), dma((nctx,)), dma((nctx,)), dma((nctx,)),
        dma((nctx,)), dma((nctx,)), dma((nctx,)), dma((nctx,)),
    ]
    teacher, loss, grad_in, grad_out = pl.pallas_call(
        functools.partial(
            kernel, nctx, nhead, kv, unit, rows * nctx, width * nhead
        ),
        out_shape=(
            jax.ShapeDtypeStruct((rows, width), BF16),
            jax.ShapeDtypeStruct((1, 1), F32),
            jax.ShapeDtypeStruct((rank, width), F32),
            jax.ShapeDtypeStruct((rank, width), BF16),
        ),
        in_specs=[vmem, vmem, vmem, pl.BlockSpec(memory_space=pl.ANY), vmem, vmem, vmem],
        out_specs=(vmem, vmem, vmem, vmem),
        scratch_shapes=scratch,
        compiler_params=pltpu.CompilerParams(
            collective_id=0, has_side_effects=True, vmem_limit_bytes=50 * 2**20
        ),
    )(queries, keys, vals, out_proj, states, adapter_in, adapter_out)
    return (teacher, loss.reshape(()), grad_in.T, grad_out.astype(F32))


def solution(mesh):
    placed = (
        P("ctx", "head"),
        P("ctx", "head", None),
        P("ctx", "head", None),
        P("ctx"),
        P("head", None),
        P("ctx", "head"),
        P("head", None),
        P(None, "head"),
    )
    return jax.shard_map(
        shards,
        mesh=mesh,
        in_specs=placed,
        out_specs=(P("ctx", "head"), P(), P("head", None), P(None, "head")),
        check_vma=False,
    )
```
